32 devices in a mesh: grp: 4 (over y, x), att: 2 (over core), dev: 4 (over z).
Axes of the slice: x: 2, y: 2, z: 4, core: 2. Of those that a mesh axis runs over, the one named last changes fastest.
Arguments:
- query: bfloat16 [8, 4, 2, 32, 1024], P(('grp', 'att'), 'dev'), parts along dimension 0, may hold values from -110 to 110
- key_cache: bfloat16 [8, 4, 2, 32, 64, 128], P(('grp', 'att'), 'dev'), parts along dimension 0, may hold values from -5.5 to 5.5
- value_cache: bfloat16 [8, 4, 2, 32, 64, 128], P(('grp', 'att'), 'dev'), parts along dimension 0, may hold values from -12 to 12
- key_new: bfloat16 [8, 4, 2, 32, 128], P(('grp', 'att'), 'dev'), parts along dimension 0, may hold values from -12 to 12
- value_new: bfloat16 [8, 4, 2, 32, 128], P(('grp', 'att'), 'dev'), parts along dimension 0, may hold values from -12 to 12
- lengths: int32 [8, 1, 2, 32], P(('grp', 'att')), parts along dimension 0, may hold values from 2 to 64, as said below
- resid: bfloat16 [8, 4, 2, 32, 1024], P(('grp', 'att'), 'dev'), parts along dimension 0, may hold values from -6 to 6
- gain: bfloat16 [4096], replicated, may hold values from 0.5 to 1.5
- w_gate: bfloat16 [4096, 14336], P(None, ('att', 'dev')), may hold values from -0.09375 to 0.09375
- w_up: bfloat16 [4096, 14336], P(None, ('att', 'dev')), may hold values from -0.09375 to 0.09375
- w_down: bfloat16 [14336, 4096], P(('att', 'dev')), may hold values from -0.0625 to 0.0625
Outputs:
- layer_out: bfloat16 [8, 4, 2, 32, 1024], P(('grp', 'att'), 'dev'), parts along dimension 0
The draws below stay inside these ranges and needn't reach their ends.
There are 4 independent parts, one for each index of `grp`. The reference program is written for one: setup_inputs(seed, part) draws one part's arguments, and reference() takes and returns one part's arrays. A program takes and returns all parts, laid end to end along the dimension named above; an argument that names none is the same for every part. Nothing has to cross between parts.
Inputs may be any that keep to these rules, and one draw needn't show every extreme that they name: `lengths`: each row's cached positions; the first row of every micro-batch of every row block holds 64.
All inputs are finite; a program needn't handle non-finite values.
Results may differ from the reference program's by a relative error of at most 0.017.
Values may be sent and summed in bfloat16 or wider, within the bound.
No kernel may reach another device: no remote copies, remote signals or barrier semaphores. Data moves between devices by JAX's collectives and lax.ppermute only.
A program may use at most 128 MiB of HBM per device.

```python
import jax
import jax.numpy as jnp
from jax import lax

HEAD_DIM = 128
KV_HEADS = 4
FF = 14336
CACHE_LEN = 64
ROWS_DEV = 32
MICRO = 2
GROUP_HEADS = 8
D = 4096
ATT_GROUPS = 2
BLOCKS = 1


def shared_keys(key):
    shape = (ATT_GROUPS, BLOCKS * KV_HEADS, MICRO, ROWS_DEV, CACHE_LEN, HEAD_DIM)
    return jnp.clip(jax.random.normal(key, shape, jnp.float32), -5.0, 5.0)


def draw_key_cache(key, part):
    cached = shared_keys(key)
    return cached.astype(jnp.bfloat16)


def draw_query(key, part):
    key = jax.random.fold_in(key, 5)
    first = jax.random.fold_in(key, 0)
    shape = (ATT_GROUPS, BLOCKS * KV_HEADS, MICRO, ROWS_DEV, GROUP_HEADS, HEAD_DIM)
    queries = jnp.clip(jax.random.normal(first, shape, jnp.float32), -5.0, 5.0)
    return queries.reshape(shape[:4] + (GROUP_HEADS * HEAD_DIM,)).astype(jnp.bfloat16)


def draw_lengths(key, part):
    key = jax.random.fold_in(key, 3)
    drawn = jax.random.randint(key, (ATT_GROUPS, BLOCKS, MICRO, ROWS_DEV), 2, CACHE_LEN + 1, jnp.int32)
    return drawn.at[..., 0].set(CACHE_LEN)


def with_spikes(result, rng, source, target, shards_of, factor):
    def block_of(position):
        return (jnp.arange(result.shape[position]) // (result.shape[position] // shards_of)).reshape((-1,) + (1,) * (result.ndim - 1 - position))

    first = jax.random.permutation(rng, shards_of)[block_of(target)]
    other_side = (block_of(target) + shards_of // 2) % shards_of
    return jnp.where((block_of(source) == first) | (block_of(source) == other_side), factor * result, result)


def block_levels(own_key, extent, cuts, least, high):
    def one(dim, shards_of):
        draws = jax.random.uniform(jax.random.fold_in(jax.random.fold_in(own_key, 6), dim), (shards_of,), jnp.float32, least / len(cuts), high / len(cuts))
        return jnp.repeat(jnp.exp(draws), extent[dim] // shards_of).reshape((-1,) + (1,) * (len(extent) - dim - 1))

    level = one(*cuts[0])
    for cut in cuts[1:]:
        level = level * one(*cut)
    return level


def scatter_about(rng, shape, scale, bound, shards=(), kind=jnp.bfloat16):
    result = scale * jax.random.normal(rng, shape, jnp.float32)
    if shards:
        result = result * block_levels(rng, shape, shards, -0.22, 0.18)
    return jnp.clip(result, -bound, bound).astype(kind)


def noise_with(rng, shape, deviation, limit, cuts, heavy, held_as=jnp.bfloat16):
    result = deviation * jax.random.normal(rng, shape, jnp.float32)
    if cuts:
        result = result * block_levels(rng, shape, cuts, -0.22, 0.18)
    return jnp.clip(with_spikes(result, jax.random.fold_in(rng, 3), *heavy), -limit, limit).astype(held_as)


def setup_inputs(seed: int = 0, part: int = 0) -> dict:
    seeds = jax.random.split(jax.random.key(seed), 12)
    own_keys = jax.random.split(jax.random.fold_in(seeds[11], part), 12)
    return {
        "query": draw_query(jax.random.fold_in(jax.random.fold_in(seeds[11], part), 71), part),
        "key_cache": draw_key_cache(jax.random.fold_in(jax.random.fold_in(seeds[11], part), 71), part),
        "value_cache": scatter_about(own_keys[2], (ATT_GROUPS, BLOCKS * KV_HEADS, MICRO, ROWS_DEV, CACHE_LEN, HEAD_DIM), 2.0, 12.0, ((0, 2), (1, 4))),
        "key_new": scatter_about(own_keys[3], (ATT_GROUPS, BLOCKS * KV_HEADS, MICRO, ROWS_DEV, HEAD_DIM), 2.0, 12.0, ((0, 2), (1, 4))),
        "value_new": scatter_about(own_keys[4], (ATT_GROUPS, BLOCKS * KV_HEADS, MICRO, ROWS_DEV, HEAD_DIM), 2.0, 12.0, ((0, 2), (1, 4))),
        "lengths": draw_lengths(jax.random.fold_in(jax.random.fold_in(seeds[11], part), 71), part),
        "resid": scatter_about(own_keys[6], (ATT_GROUPS, BLOCKS * KV_HEADS, MICRO, ROWS_DEV, GROUP_HEADS * HEAD_DIM), 1.0, 6.0, ((0, 2), (1, 4))),
        "gain": jnp.clip(jax.random.uniform(seeds[7], (D,), jnp.float32, 0.5, 1.5), 0.5, 1.5).astype(jnp.bfloat16),
        "w_gate": scatter_about(seeds[8], (D, FF), D ** -0.5, 0.09375, ((1, 8),)),
        "w_up": scatter_about(seeds[9], (D, FF), D ** -0.5, 0.09375, ((1, 8),)),
        "w_down": noise_with(seeds[10], (FF, D), FF ** -0.5, 0.0625, ((0, 8),), (0, 1, 8, 2.0)),
    }


def attend(query, key_cache, value_cache, key_new, value_new, row_lengths):
    head_dim = key_cache.shape[-1]
    grouped = query.astype(jnp.float32).reshape(query.shape[:-1] + (query.shape[-1] // head_dim, head_dim))
    score_scale = head_dim ** (-0.5)
    cached = jnp.einsum('...gc,...tc->...gt', grouped, key_cache.astype(jnp.float32)) * score_scale
    fresh = jnp.einsum('...gc,...c->...g', grouped, key_new.astype(jnp.float32)) * score_scale
    positions = jnp.arange(key_cache.shape[-2], dtype=jnp.int32)
    valid = positions < row_lengths[..., None, None]
    cached = jnp.where(valid, cached, -1e+30)
    row_max = jnp.maximum(lax.optimization_barrier(jnp.max(cached, axis=-1)), fresh)
    weights = jnp.where(valid, jnp.exp(cached - row_max[..., None]), 0.0)
    own_weight = jnp.exp(fresh - row_max)
    total = lax.optimization_barrier(jnp.sum(weights, axis=-1)) + own_weight
    probs = (weights / total[..., None]).astype(jnp.bfloat16)
    own_prob = (own_weight / total).astype(jnp.bfloat16)
    attended = jnp.einsum('...gt,...tc->...gc', probs.astype(jnp.float32), value_cache.astype(jnp.float32))
    attended = attended + own_prob.astype(jnp.float32)[..., None] * value_new.astype(jnp.float32)[..., None, :]
    return attended.reshape(query.shape)

def reference(query, key_cache, value_cache, key_new, value_new, lengths, resid, gain, w_gate, w_up, w_down):
    row_lengths = jnp.repeat(lengths, KV_HEADS, axis=1)
    attended = attend(query, key_cache, value_cache, key_new, value_new, row_lengths)
    stream = (resid.astype(jnp.float32) + attended).astype(jnp.bfloat16)
    width = GROUP_HEADS * HEAD_DIM
    blocked = stream.reshape(ATT_GROUPS, BLOCKS, KV_HEADS, MICRO, ROWS_DEV, width)
    widened = blocked.astype(jnp.float32)
    mean_square = lax.optimization_barrier(jnp.mean(widened * widened, axis=(2, 5), keepdims=True))
    gain_rows = gain.astype(jnp.float32).reshape(1, 1, KV_HEADS, 1, 1, width)
    normed = (widened * lax.rsqrt(mean_square + 1e-05) * gain_rows).astype(jnp.bfloat16)
    normed_wide = normed.astype(jnp.float32)
    gate = jnp.einsum('abkmrc,kcf->abmrf', normed_wide, w_gate.astype(jnp.float32).reshape(KV_HEADS, width, FF))
    up_part = jnp.einsum('abkmrc,kcf->abmrf', normed_wide, w_up.astype(jnp.float32).reshape(KV_HEADS, width, FF))
    hidden = (jax.nn.silu(gate) * up_part).astype(jnp.bfloat16)
    summed = jnp.einsum('abmrf,fkc->abkmrc', hidden.astype(jnp.float32), w_down.astype(jnp.float32).reshape(FF, KV_HEADS, width))
    layer_out = (widened + summed).astype(jnp.bfloat16)
    return layer_out.reshape(ATT_GROUPS, BLOCKS * KV_HEADS, MICRO, ROWS_DEV, width)
```

```python
import functools

import jax
import jax.numpy as jnp
from jax import lax
from jax.experimental import pallas as pl
from jax.experimental.pallas import tpu as pltpu
from jax.sharding import PartitionSpec as P

KV_HEADS = 4
MIB = 1 << 20
LONG = 20000000000
LOG2E = 1.4426950408889634
PREP = 3000000000
COSTS = (LONG, 2000000000)
VMEM = pl.BlockSpec(memory_space=pltpu.VMEM)
HBM = pl.BlockSpec(memory_space=pltpu.HBM)


def params(limit=2 * MIB):
    return pltpu.CompilerParams(vmem_limit_bytes=limit)


def in_hbm(x):
    return pltpu.with_memory_space_constraint(x, pltpu.HBM)


def cost(flops, bytes_accessed):
    return pl.CostEstimate(flops=flops, bytes_accessed=bytes_accessed, transcendentals=0)


def peer(offset):
    return lax.axis_index("dev") ^ offset


def head_start(offset, width):
    return pl.multiple_of(lax.rem(peer(offset), KV_HEADS) * width, width)


def block_start(devices, offset, rows):
    if devices == KV_HEADS:
        return 0
    return pl.multiple_of(peer(offset) // KV_HEADS * rows, rows)


def column_tiles(units, tile=256):
    return [slice(c, min(c + tile, units)) for c in range(0, units, tile)]


def attend_rows(len_of, relative, q_ref, k_ref, v_ref, kn_ref, vn_ref, res_ref):
    part, width = q_ref.shape
    head = kn_ref.shape[-1]
    heads = width // head
    groups = part // 8
    span = k_ref.shape[0] // groups
    factor = head ** (-0.5) * LOG2E
    sub = lax.broadcasted_iota(jnp.int32, (8, 128), 0)
    wide = q_ref[...].astype(jnp.float32)
    fresh_keys = kn_ref[...].astype(jnp.float32)
    fresh_values = vn_ref[...].astype(jnp.float32)
    spread, keys_spread, biases = [], [], []
    for g in range(groups):
        own = slice(8 * g, 8 * g + 8)
        spread += [wide[own, i * head : (i + 1) * head] for i in range(heads)]
        keys_spread += [fresh_keys[own]] * heads
        limit = jnp.zeros((8, 128), jnp.int32)
        for r in range(8):
            limit = jnp.where(sub == r, len_of(8 * g + r), limit)
        limit = jnp.concatenate([limit] * (span // 128), axis=1)
        bias = jnp.where(relative < limit, 0.0, -1e30)
        biases.append(jnp.concatenate([bias] * heads, axis=0))
    q = jnp.concatenate(spread, axis=0)
    fresh = jnp.sum(q * jnp.concatenate(keys_spread, axis=0), axis=-1, keepdims=True)
    q = q.astype(jnp.bfloat16)
    scores = []
    for g in range(groups):
        scores.append(
            lax.dot_general(
                q[8 * heads * g : 8 * heads * (g + 1)],
                k_ref[g * span : (g + 1) * span, :],
                (((1,), (1,)), ((), ())),
                preferred_element_type=jnp.float32,
            )
            + biases[g]
        )
    scores = jnp.concatenate(scores, axis=0)
    top = jnp.maximum(jnp.max(scores, axis=-1, keepdims=True), fresh)
    weights = jnp.exp2((scores - top) * factor)
    own_weight = jnp.exp2((fresh - top) * factor)
    inverse = 1.0 / (jnp.sum(weights, axis=-1, keepdims=True) + own_weight)
    own_weight = own_weight * inverse
    weights = weights.astype(jnp.bfloat16)
    rows = []
    for g in range(groups):
        mine = slice(8 * heads * g, 8 * heads * (g + 1))
        attended = jnp.dot(weights[mine], v_ref[g * span : (g + 1) * span, :], preferred_element_type=jnp.float32)
        own = jnp.concatenate([fresh_values[8 * g : 8 * g + 8]] * heads, axis=0)
        attended = attended * inverse[mine] + own_weight[mine] * own
        rows.append(jnp.concatenate([attended[8 * i : 8 * i + 8] for i in range(heads)], axis=1))
    return (res_ref[...].astype(jnp.float32) + jnp.concatenate(rows, axis=0)).astype(jnp.bfloat16)


def relative_positions(cache):
    lane = lax.broadcasted_iota(jnp.int32, (8, 8 * cache), 1)
    relative = lane - cache * lax.broadcasted_iota(jnp.int32, (8, 8 * cache), 0)
    return jnp.where(relative < 0, cache, relative)


def attend_kernel(devices, batch, len_in, *refs):
    count = 6
    sources, out_ref, refs = refs[:count], refs[count], refs[count + 1 :]
    if batch == 0:
        later, refs = refs[:count], refs[count:]
        sources_later = sources
        held, refs = refs[:count], refs[count:]
    else:
        held, later = sources, ()
    len_ref, sem = refs
    block = lax.axis_index("dev") // KV_HEADS if devices > KV_HEADS else 0
    lengths = pltpu.make_async_copy(len_in, len_ref, sem.at[2 * count])
    lengths.start()
    copies = []
    if batch == 0:
        for n in (0, 3, 1, 2, 4, 5):
            rows = held[n].shape[0]
            copies.append(pltpu.make_async_copy(sources[n].at[pl.ds(0, rows)], held[n], sem.at[n]))
        for n in (1, 2, 0, 3, 4, 5):
            rows = held[n].shape[0]
            copies.append(pltpu.make_async_copy(sources_later[n].at[pl.ds(rows, rows)], later[n], sem.at[count + n]))
        for copy in copies:
            copy.start()
    cache = held[1].shape[0] // held[0].shape[0]
    relative = relative_positions(cache)
    lengths.wait()
    for copy in copies[:count]:
        copy.wait()
    out_ref[...] = attend_rows(lambda r: len_ref[block, batch, r], relative, *held)
    for copy in copies[count:]:
        copy.wait()


def attend(devices, batch, lengths, *arrays):
    rows = arrays[0].shape[0] // (2 if batch == 0 else 1)
    width = arrays[0].shape[1]
    shapes = [pltpu.VMEM((rows, width), jnp.bfloat16)]
    scratch = []
    if batch == 0:
        halves = [(a.shape[0] // 2,) + a.shape[1:] for a in arrays]
        shapes += [pltpu.VMEM(shape, a.dtype) for shape, a in zip(halves, arrays)]
        scratch = [pltpu.VMEM(shape, a.dtype) for shape, a in zip(halves, arrays)]
    return pl.pallas_call(
        functools.partial(attend_kernel, devices, batch),
        out_shape=shapes,
        in_specs=[HBM] + [HBM if batch == 0 else VMEM] * len(arrays),
        out_specs=[VMEM] * len(shapes),
        scratch_shapes=scratch
        + [pltpu.SMEM(lengths.shape, lengths.dtype), pltpu.SemaphoreType.DMA((2 * len(arrays) + 1,))],
        compiler_params=params(4 * MIB),
        cost_estimate=cost(COSTS[batch], 0),
        name="attend",
    )(lengths, *arrays)


def silu_product(gate, up):
    return (gate / (1.0 + jnp.exp(-gate)) * up).astype(jnp.bfloat16)


def place_rows(devices, offsets, pieces, x_ref):
    rows, width = pieces[0].shape
    for n, offset in enumerate(offsets):
        lanes = pl.ds(head_start(offset, width), width)
        part = pl.ds(block_start(devices, offset, rows), rows)
        for side in range(2):
            x_ref[side, part, lanes] = pieces[2 * n + side][...]


def normalize(x_ref, gain_ref, out_ref):
    gain = gain_ref[...].astype(jnp.float32).reshape(1, gain_ref.shape[0])
    for side in range(2):
        for part in range(x_ref.shape[1] // 16):
            stripe = slice(16 * part, 16 * part + 16)
            x = x_ref[side, stripe, :].astype(jnp.float32)
            inverse = lax.rsqrt(jnp.mean(x * x, axis=-1, keepdims=True) + 1e-05)
            out_ref[side, stripe, :] = (x * inverse * gain).astype(jnp.bfloat16)


def prepare_kernel(devices, offsets, gain_ref, *refs):
    pieces, (out_ref, x_ref) = refs[:-2], refs[-2:]
    place_rows(devices, offsets, pieces, x_ref)
    normalize(x_ref, gain_ref, out_ref)


def prepare(devices, offsets, pieces, gain):
    rows, width = pieces[0].shape
    blocks = devices // KV_HEADS
    shape = (2, blocks * rows, KV_HEADS * width)
    return pl.pallas_call(
        functools.partial(prepare_kernel, devices, offsets),
        out_shape=pltpu.VMEM(shape, jnp.bfloat16),
        in_specs=[VMEM] * (1 + len(pieces)),
        out_specs=VMEM,
        scratch_shapes=[pltpu.VMEM(shape, jnp.bfloat16)],
        compiler_params=params(blocks * 2 * MIB),
        cost_estimate=cost(PREP, 0),
        name="prepare",
    )(gain, *pieces)


def hidden_kernel(devices, offsets, gain_ref, wg_ref, wu_ref, wd_ref, ready_ref, *refs):
    del wd_ref
    pieces, (hidden_ref, late_ref, x_ref) = refs[:-3], refs[-3:]
    rows, _ = pieces[0].shape
    total, units = hidden_ref.shape
    place_rows(devices, offsets, pieces, late_ref)
    normalize(late_ref, gain_ref, late_ref)
    for block in range(devices // KV_HEADS):
        part = slice(block * rows, (block + 1) * rows)
        for side in range(2):
            for batch, ref in enumerate((ready_ref, late_ref)):
                row = (4 * block + 2 * side + batch) * rows
                x_ref[row : row + rows, :] = ref[side, part, :]
    x = x_ref[...]
    for lanes in column_tiles(units):
        gate = jnp.dot(x, wg_ref[:, lanes], preferred_element_type=jnp.float32)
        up = jnp.dot(x, wu_ref[:, lanes], preferred_element_type=jnp.float32)
        hidden_ref[:, lanes] = silu_product(gate, up)


def hidden_units(devices, offsets, ready, pieces, gain, w_gate, w_up, w_down):
    features, units = w_gate.shape
    total = 2 * ready.shape[0] * ready.shape[1]
    return pl.pallas_call(
        functools.partial(hidden_kernel, devices, offsets),
        out_shape=pltpu.VMEM((total, units), jnp.bfloat16),
        in_specs=[VMEM] * (5 + len(pieces)),
        out_specs=VMEM,
        scratch_shapes=[pltpu.VMEM(ready.shape, jnp.bfloat16), pltpu.VMEM((total, features), jnp.bfloat16)],
        compiler_params=params(devices // KV_HEADS * 5 * MIB),
        cost_estimate=cost(4 * total * features * units, 0),
        name="hidden",
    )(gain, w_gate, w_up, w_down, ready, *pieces)


def down_kernel(devices, offsets, hidden_ref, weight_ref, *refs):
    keep_ref, send_ref = refs[-2:]
    _, rows, width = keep_ref.shape
    for n, offset in enumerate(offsets):
        mine = pl.ds(block_start(devices, offset, 2 * rows), 2 * rows)
        hidden = hidden_ref[mine, :]
        for lanes in column_tiles(width):
            size = lanes.stop - lanes.start
            column = pl.multiple_of(head_start(offset, width) + lanes.start, size)
            term = jnp.dot(hidden, weight_ref[:, pl.ds(column, size)], preferred_element_type=jnp.float32)
            keep_ref[n, :, lanes] = term[:rows]
            send_ref[n, :, lanes] = term[rows:].astype(jnp.bfloat16)


def down(devices, offsets, hidden, w_down, rows, after=()):
    units, features = w_down.shape
    width = features // KV_HEADS
    shape = (len(offsets), rows, width)
    return pl.pallas_call(
        functools.partial(down_kernel, devices, offsets),
        out_shape=[pltpu.VMEM(shape, jnp.float32), pltpu.VMEM(shape, jnp.bfloat16)],
        in_specs=[VMEM] * 2 + [pl.BlockSpec(memory_space=pl.ANY)] * len(after),
        out_specs=[VMEM] * 2,
        compiler_params=params(),
        cost_estimate=cost(4 * rows * width * units * len(offsets), 0),
        name="down",
    )(hidden, w_down, *after)


def fold_kernel(offsets, count, *refs):
    keep_ref, got_ref = refs[:2]
    more, out_refs = refs[2 : 2 + count], refs[-len(offsets) :]
    for n, out_ref in enumerate(out_refs):
        term = keep_ref[n] + got_ref[n].astype(jnp.float32)
        for ref in more:
            term = term + ref[...].astype(jnp.float32)
        out_ref[...] = term.astype(out_ref.dtype)


def fold(offsets, keep, got, more=(), after=(), flops=0):
    _, rows, width = keep.shape
    return pl.pallas_call(
        functools.partial(fold_kernel, offsets, len(more)),
        out_shape=[pltpu.VMEM((rows, width), jnp.float32 if o == 0 else jnp.bfloat16) for o in offsets],
        in_specs=[VMEM] * (2 + len(more)) + [pl.BlockSpec(memory_space=pl.ANY)] * len(after),
        out_specs=[VMEM] * len(offsets),
        compiler_params=params(),
        cost_estimate=cost(flops, 0),
        name="fold",
    )(keep, got, *more, *after)


def finish_kernel(first_ref, second_ref, *refs):
    out_ref = refs[-1]
    rows = first_ref.shape[0]
    for n, stream_ref in enumerate((first_ref, second_ref)):
        part = slice(n * rows, (n + 1) * rows)
        total = stream_ref[...].astype(jnp.float32)
        for ref in refs[:-1]:
            total = total + ref[part, :].astype(jnp.float32)
        out_ref[part, :] = total.astype(out_ref.dtype)


def finish(streams, terms):
    return pl.pallas_call(
        finish_kernel,
        out_shape=jax.ShapeDtypeStruct(terms[0].shape, jnp.bfloat16),
        compiler_params=params(),
        name="finish",
    )(*streams, *terms)


def swap(x):
    return lax.ppermute(x, "att", [(0, 1), (1, 0)])


def exchange(x, offset, devices):
    return lax.ppermute(x, "dev", [(i, i ^ offset) for i in range(devices)])


def shards(
    query, key_cache, value_cache, key_new, value_new, lengths, resid, gain, w_gate, w_up, w_down
):
    devices = lax.axis_size("dev")
    width = query.shape[-1]
    head = key_cache.shape[-1]
    lengths = in_hbm(lengths[0])
    first, *rest = attend(
        devices,
        0,
        lengths,
        in_hbm(query.reshape(-1, width)),
        in_hbm(key_cache.reshape(-1, head)),
        in_hbm(value_cache.reshape(-1, head)),
        in_hbm(key_new.reshape(-1, head)),
        in_hbm(value_new.reshape(-1, head)),
        in_hbm(resid.reshape(-1, width)),
    )
    (second,) = attend(devices, 1, lengths, *rest)
    streams = (first, second)
    rows = 2 * first.shape[0]
    offsets = tuple(range(devices))
    arrived = []
    for stream in streams:
        pieces = {0: stream}
        bit = devices // 2
        while bit:
            for o in tuple(pieces):
                pieces[o ^ bit] = exchange(pieces[o], bit, devices)
            bit //= 2
        arrived.append([x for o in offsets for x in (pieces[o], swap(pieces[o]))])
    ready = prepare(devices, offsets, arrived[0], gain)
    hidden = hidden_units(devices, offsets, ready, arrived[1], gain, w_gate, w_up, w_down)

    def part(offsets, after=()):
        keep, send = down(devices, offsets, hidden, w_down, rows, after)
        return offsets, keep, swap(send)

    if devices == 4:
        (third,) = fold(*part((3,)))
        relayed = exchange(third, 1, devices)
        second_parts = part((2,))
        nearer_parts = part((1, 0), (third,))
        (second,) = fold(*second_parts, (relayed,), (), LONG)
        first, own = fold(*nearer_parts, (), (second,))
        terms = [own, exchange(first, 1, devices), exchange(second, 2, devices)]
    else:
        terms = {}
        for start in range(devices - 2, -1, -2):
            offsets = (start + 1, start)
            for o, term in zip(offsets, fold(*part(offsets))):
                terms[o] = term if o == 0 else exchange(term, o, devices)
        terms = [terms[o] for o in range(devices)]
    return finish(streams, terms).reshape(query.shape)


def solution(mesh):
    return jax.shard_map(
        shards,
        mesh=mesh,
        in_specs=(
            P(("grp", "att"), "dev", None, None, None),
            P(("grp", "att"), "dev", None, None, None, None),
            P(("grp", "att"), "dev", None, None, None, None),
            P(("grp", "att"), "dev", None, None, None),
            P(("grp", "att"), "dev", None, None, None),
            P(("grp", "att"), None, None, None),
            P(("grp", "att"), "dev", None, None, None),
            P(),
            P(None, ("att", "dev")),
            P(None, ("att", "dev")),
            P(("att", "dev"), None),
        ),
        out_specs=P(("grp", "att"), "dev", None, None, None),
        check_vma=False,
    )
```

```python
import functools

import jax
import jax.numpy as jnp
from jax import lax
from jax.experimental import pallas as pl
from jax.experimental.pallas import tpu as pltpu
from jax.sharding import PartitionSpec as P

KV_HEADS = 4
MIB = 1 << 20
LONG = 20000000000
ATTC = 3 * LONG
RELC = 0
STAGEC = 1000000000
DOWNC = 10000000000
SLIM = 4
LOG2E = 1.4426950408889634
VMEM = pl.BlockSpec(memory_space=pltpu.VMEM)
HBM = pl.BlockSpec(memory_space=pltpu.HBM)


def params(limit=1 * MIB):
    return pltpu.CompilerParams(vmem_limit_bytes=limit)


def in_hbm(x):
    return pltpu.with_memory_space_constraint(x, pltpu.HBM)


def cost(flops, bytes_accessed):
    return pl.CostEstimate(flops=flops, bytes_accessed=bytes_accessed, transcendentals=0)


def peer(offset):
    return lax.axis_index("dev") ^ offset


def head_start(offset, width):
    return pl.multiple_of(lax.rem(peer(offset), KV_HEADS) * width, width)


def block_start(devices, offset, rows):
    if devices == KV_HEADS:
        return 0
    return pl.multiple_of(peer(offset) // KV_HEADS * rows, rows)


def column_tiles(units, tile=256):
    return [slice(c, min(c + tile, units)) for c in range(0, units, tile)]


def attend_kernel(devices, len_in, q_in, k_in, v_in, kn_in, vn_in, res_in, out_ref, *scratch):
    len_ref, q_ref, k_ref, v_ref, kn_ref, vn_ref, res_ref, len_sem, small_sem, cache_sem = scratch
    rows, width = q_ref.shape
    head = kn_ref.shape[-1]
    heads = width // head
    cache = k_ref.shape[0] // rows
    halves = cache_sem.shape[1]
    part = rows // halves
    groups = part // 8
    block = lax.axis_index("dev") // KV_HEADS if devices > KV_HEADS else 0
    per_batch = len_ref.shape[-1]
    factor = head ** (-0.5) * LOG2E

    lengths = pltpu.make_async_copy(len_in, len_ref, len_sem)
    small = [
        pltpu.make_async_copy(source, target, small_sem.at[n])
        for n, (source, target) in enumerate(((q_in, q_ref), (kn_in, kn_ref), (vn_in, vn_ref), (res_in, res_ref)))
    ]
    cached = []
    for h in range(halves):
        span = pl.ds(h * part * cache, part * cache)
        cached.append(
            [
                pltpu.make_async_copy(source.at[span], target.at[span], cache_sem.at[n, h])
                for n, (source, target) in enumerate(((k_in, k_ref), (v_in, v_ref)))
            ]
        )
    lengths.start()
    small[0].start()
    small[1].start()
    for pair in cached:
        for copy in pair:
            copy.start()
    small[2].start()
    small[3].start()

    relative = lax.broadcasted_iota(jnp.int32, (8, 8 * cache), 1)
    relative = relative - cache * lax.broadcasted_iota(jnp.int32, (8, 8 * cache), 0)
    relative = jnp.where(relative < 0, cache, relative)
    sub = lax.broadcasted_iota(jnp.int32, (8, 128), 0)
    lengths.wait()
    small[0].wait()
    small[1].wait()
    for h in range(halves):
        stripe = slice(h * part, (h + 1) * part)
        wide = q_ref[stripe, :].astype(jnp.float32)
        fresh_keys = kn_ref[stripe, :].astype(jnp.float32)
        spread, keys_spread, biases = [], [], []
        for g in range(groups):
            own = slice(8 * g, 8 * g + 8)
            spread += [wide[own, i * head : (i + 1) * head] for i in range(heads)]
            keys_spread += [fresh_keys[own]] * heads
            limit = jnp.zeros((8, 128), jnp.int32)
            for r in range(8):
                row = h * part + 8 * g + r
                limit = jnp.where(sub == r, len_ref[block, row // per_batch, row % per_batch], limit)
            limit = jnp.concatenate([limit] * (8 * cache // 128), axis=1)
            bias = jnp.where(relative < limit, 0.0, -1e30)
            biases.append(jnp.concatenate([bias] * heads, axis=0))
        q = jnp.concatenate(spread, axis=0)
        fresh = jnp.sum(q * jnp.concatenate(keys_spread, axis=0), axis=-1, keepdims=True)
        q = q.astype(jnp.bfloat16)
        if h == 0:
            small[2].wait()
            small[3].wait()
        for copy in cached[h]:
            copy.wait()
        scores = []
        span = 8 * cache
        for g in range(groups):
            first = (h * groups + g) * span
            scores.append(
                lax.dot_general(
                    q[8 * heads * g : 8 * heads * (g + 1)],
                    k_ref[first : first + span, :],
                    (((1,), (1,)), ((), ())),
                    preferred_element_type=jnp.float32,
                )
                + biases[g]
            )
        scores = jnp.concatenate(scores, axis=0)
        top = jnp.maximum(jnp.max(scores, axis=-1, keepdims=True), fresh)
        weights = jnp.exp2((scores - top) * factor)
        own_weight = jnp.exp2((fresh - top) * factor)
        inverse = 1.0 / (jnp.sum(weights, axis=-1, keepdims=True) + own_weight)
        own_weight = own_weight * inverse
        weights = weights.astype(jnp.bfloat16)
        for g in range(groups):
            first = (h * groups + g) * span
            block_rows = slice(8 * heads * g, 8 * heads * (g + 1))
            attended = jnp.dot(
                weights[block_rows], v_ref[first : first + span, :], preferred_element_type=jnp.float32
            )
            attended = attended * inverse[block_rows]
            own = slice(h * part + 8 * g, h * part + 8 * g + 8)
            fresh_values = vn_ref[h * part : (h + 1) * part, :].astype(jnp.float32)[8 * g : 8 * g + 8]
            attended = attended + own_weight[block_rows] * jnp.concatenate([fresh_values] * heads, axis=0)
            spread[g] = jnp.concatenate([attended[8 * i : 8 * i + 8] for i in range(heads)], axis=1)
        attended = jnp.concatenate(spread[:groups], axis=0)
        out_ref[stripe, :] = (res_ref[stripe, :].astype(jnp.float32) + attended).astype(out_ref.dtype)


def attend(devices, lengths, *arrays):
    query, keys = arrays[:2]
    rows, width = query.shape
    halves = 2
    return pl.pallas_call(
        functools.partial(attend_kernel, devices),
        out_shape=pltpu.VMEM((rows, width), jnp.bfloat16),
        in_specs=[HBM] * (1 + len(arrays)),
        out_specs=VMEM,
        scratch_shapes=[pltpu.SMEM(lengths.shape, lengths.dtype)]
        + [pltpu.VMEM(a.shape, a.dtype) for a in arrays]
        + [
            pltpu.SemaphoreType.DMA,
            pltpu.SemaphoreType.DMA((4,)),
            pltpu.SemaphoreType.DMA((2, halves)),
        ],
        compiler_params=params(5 * MIB),
        cost_estimate=cost(ATTC, 0),
        name="attend",
    )(lengths, *arrays)


def silu_product(gate, up):
    return (gate / (1.0 + jnp.exp(-gate)) * up).astype(jnp.bfloat16)


def stage_kernel(devices, offsets, first, last, gain_ref, wg_ref, wu_ref, *refs):
    pieces, refs = refs[: 2 * len(offsets)], refs[2 * len(offsets) :]
    if not first:
        gate_in, up_in, square_in = refs[:3]
        refs = refs[3:]
    if last:
        hidden_ref, x_ref = refs[-2:]
    else:
        gate_out, up_out, square_out, x_ref = refs
    rows, width = pieces[0].shape
    units = wg_ref.shape[1]
    many = devices > KV_HEADS
    if many and first:
        for ref in (gate_out, up_out, square_out):
            ref[...] = jnp.zeros_like(ref)
    if many and last:
        gate_out, up_out, square_out = gate_in, up_in, square_in
    if many:
        gate_in, up_in, square_in = gate_out, up_out, square_out
    places, squares = [], []
    for n, offset in enumerate(offsets):
        depth = pl.ds(head_start(offset, width), width)
        places.append((pl.ds(block_start(devices, offset, 2 * rows), 2 * rows), depth))
        gain = gain_ref[depth].astype(jnp.float32).reshape(1, width)
        sums = []
        for side in range(2):
            x = pieces[2 * n + side][...].astype(jnp.float32)
            x_ref[n, side * rows : (side + 1) * rows, :] = (x * gain).astype(jnp.bfloat16)
            sums.append(jnp.sum(x * x, axis=-1, keepdims=True))
        squares.append(jnp.broadcast_to(jnp.concatenate(sums, axis=0), (2 * rows, 128)))

    def product(n, weight, lanes):
        return jnp.dot(x_ref[n], weight[places[n][1], lanes], preferred_element_type=jnp.float32)

    if many:
        for n in range(len(offsets)):
            mine = places[n][0]
            square_out[mine, :] += squares[n]
            for lanes in column_tiles(units):
                gate_out[mine, lanes] += product(n, wg_ref, lanes)
                up_out[mine, lanes] += product(n, wu_ref, lanes)
        if last:
            inverse = lax.rsqrt(square_in[:, :1] / (KV_HEADS * width) + 1e-05)
            for lanes in column_tiles(units):
                hidden_ref[:, lanes] = silu_product(gate_in[:, lanes] * inverse, up_in[:, lanes] * inverse)
        return
    square = sum(squares[1:], squares[0])
    if not first:
        square = square + square_in[...]
    if last:
        inverse = lax.rsqrt(square[:, :1] / (KV_HEADS * width) + 1e-05)
    else:
        square_out[...] = square
    for lanes in column_tiles(units):
        gate = sum(product(n, wg_ref, lanes) for n in range(len(offsets)))
        up = sum(product(n, wu_ref, lanes) for n in range(len(offsets)))
        if not first:
            gate = gate + gate_in[:, lanes]
            up = up + up_in[:, lanes]
        if last:
            hidden_ref[:, lanes] = silu_product(gate * inverse, up * inverse)
        else:
            gate_out[:, lanes] = gate
            up_out[:, lanes] = up


def stage(devices, offsets, pieces, gain, w_gate, w_up, state, final, present):
    rows, width = pieces[0].shape
    units = w_gate.shape[1]
    total = devices // KV_HEADS * 2 * rows
    first, last = not state, final
    arguments = [gain, w_gate, w_up] + list(pieces) + list(state)
    if final:
        arguments += present
    aliases = {}
    if last:
        shapes = [pltpu.VMEM((total, units), jnp.bfloat16)]
    else:
        shapes = [
            pltpu.VMEM((total, units), jnp.float32),
            pltpu.VMEM((total, units), jnp.float32),
            pltpu.VMEM((total, 128), jnp.float32),
        ]
        if not first:
            aliases = {len(arguments) - 3 + n: n for n in range(3)}
    return pl.pallas_call(
        functools.partial(stage_kernel, devices, offsets, first, last),
        out_shape=shapes,
        in_specs=[VMEM] * len(arguments),
        out_specs=[VMEM] * len(shapes),
        input_output_aliases=aliases,
        scratch_shapes=[pltpu.VMEM((len(offsets), 2 * rows, width), jnp.bfloat16)],
        compiler_params=params(devices // KV_HEADS * SLIM * MIB),
        cost_estimate=cost(STAGEC, 0),
        name="stage",
    )(*arguments)


def relay_kernel(piece_ref, *refs):
    refs[-1][...] = piece_ref[...]


def relay(piece, after, present):
    return pl.pallas_call(
        relay_kernel,
        out_shape=pltpu.VMEM(piece.shape, piece.dtype),
        in_specs=[VMEM] + [pl.BlockSpec(memory_space=pl.ANY)] * len(after) + [VMEM] * len(present),
        out_specs=VMEM,
        compiler_params=params(),
        cost_estimate=cost(RELC, 0),
        name="relay",
    )(piece, *after, *present)


def down_kernel(devices, offsets, hidden_ref, weight_ref, *refs):
    keep_ref, send_ref = refs[-2:]
    _, rows, width = keep_ref.shape
    for n, offset in enumerate(offsets):
        mine = pl.ds(block_start(devices, offset, 2 * rows), 2 * rows)
        hidden = hidden_ref[mine, :]
        for lanes in column_tiles(width):
            size = lanes.stop - lanes.start
            column = pl.multiple_of(head_start(offset, width) + lanes.start, size)
            term = jnp.dot(hidden, weight_ref[:, pl.ds(column, size)], preferred_element_type=jnp.float32)
            keep_ref[n, :, lanes] = term[:rows]
            send_ref[n, :, lanes] = term[rows:].astype(jnp.bfloat16)


def down(devices, offsets, hidden, w_down, rows, after=()):
    units, features = w_down.shape
    width = features // KV_HEADS
    shape = (len(offsets), rows, width)
    return pl.pallas_call(
        functools.partial(down_kernel, devices, offsets),
        out_shape=[pltpu.VMEM(shape, jnp.float32), pltpu.VMEM(shape, jnp.bfloat16)],
        in_specs=[VMEM] * 2 + [pl.BlockSpec(memory_space=pl.ANY)] * len(after),
        out_specs=[VMEM] * 2,
        compiler_params=params(),
        cost_estimate=cost(DOWNC, 0),
        name="down",
    )(hidden, w_down, *after)


def fold_kernel(offsets, count, *refs):
    keep_ref, got_ref = refs[:2]
    more, out_refs = refs[2 : 2 + count], refs[-len(offsets) :]
    for n, out_ref in enumerate(out_refs):
        term = keep_ref[n] + got_ref[n].astype(jnp.float32)
        for ref in more:
            term = term + ref[...].astype(jnp.float32)
        out_ref[...] = term.astype(out_ref.dtype)


def fold(offsets, keep, got, more=(), after=(), flops=0):
    _, rows, width = keep.shape
    return pl.pallas_call(
        functools.partial(fold_kernel, offsets, len(more)),
        out_shape=[pltpu.VMEM((rows, width), jnp.float32 if o == 0 else jnp.bfloat16) for o in offsets],
        in_specs=[VMEM] * (2 + len(more)) + [pl.BlockSpec(memory_space=pl.ANY)] * len(after),
        out_specs=[VMEM] * len(offsets),
        compiler_params=params(),
        cost_estimate=cost(flops, 0),
        name="fold",
    )(keep, got, *more, *after)


def finish_kernel(stream_ref, *refs):
    out_ref = refs[-1]
    total = stream_ref[...].astype(jnp.float32)
    for ref in refs[:-1]:
        total = total + ref[...].astype(jnp.float32)
    out_ref[...] = total.astype(out_ref.dtype)


def finish(stream, terms):
    return pl.pallas_call(
        finish_kernel,
        out_shape=jax.ShapeDtypeStruct(stream.shape, jnp.bfloat16),
        compiler_params=params(),
        name="finish",
    )(stream, *terms)


def swap(x):
    return lax.ppermute(x, "att", [(0, 1), (1, 0)])


def exchange(x, offset, devices):
    return lax.ppermute(x, "dev", [(i, i ^ offset) for i in range(devices)])


def shards(
    query, key_cache, value_cache, key_new, value_new, lengths, resid, gain, w_gate, w_up, w_down
):
    devices = lax.axis_size("dev")
    width = query.shape[-1]
    head = key_cache.shape[-1]
    stream = attend(
        devices,
        in_hbm(lengths[0]),
        in_hbm(query.reshape(-1, width)),
        in_hbm(key_cache.reshape(-1, head)),
        in_hbm(value_cache.reshape(-1, head)),
        in_hbm(key_new.reshape(-1, head)),
        in_hbm(value_new.reshape(-1, head)),
        in_hbm(resid.reshape(-1, width)),
    )
    rows = stream.shape[0]
    pieces = {0: stream}
    bit = devices // 2
    while bit:
        for o in tuple(pieces):
            pieces[o ^ bit] = exchange(pieces[o], bit, devices)
        bit //= 2
    groups = [(0,), (2, 1), (3,)] if devices == 4 else [(o,) for o in range(devices)]
    state = ()
    for group in groups:
        arrived = []
        for o in group:
            piece = pieces[o]
            if state and group is groups[-1]:
                piece = relay(piece, state[2:], [w_down])
            elif state:
                piece = relay(piece, state[2:], [])
            arrived += [piece, swap(piece)]
        state = stage(devices, group, arrived, gain, w_gate, w_up, state, group is groups[-1], [])
    hidden = state[0]

    def part(offsets, after=()):
        keep, send = down(devices, offsets, hidden, w_down, rows, after)
        return offsets, keep, swap(send)

    if devices == 4:
        (third,) = fold(*part((3,)))
        relayed = exchange(third, 1, devices)
        second_parts = part((2,))
        nearer_parts = part((1, 0), (third,))
        (second,) = fold(*second_parts, (relayed,), (), LONG)
        first, own = fold(*nearer_parts, (), (second,))
        terms = [own, exchange(first, 1, devices), exchange(second, 2, devices)]
    else:
        terms = {}
        for start in range(devices - 2, -1, -2):
            offsets = (start + 1, start)
            for o, term in zip(offsets, fold(*part(offsets))):
                terms[o] = term if o == 0 else exchange(term, o, devices)
        terms = [terms[o] for o in range(devices)]
    return finish(stream, terms).reshape(query.shape)


def solution(mesh):
    return jax.shard_map(
        shards,
        mesh=mesh,
        in_specs=(
            P(("grp", "att"), "dev", None, None, None),
            P(("grp", "att"), "dev", None, None, None, None),
            P(("grp", "att"), "dev", None, None, None, None),
            P(("grp", "att"), "dev", None, None, None),
            P(("grp", "att"), "dev", None, None, None),
            P(("grp", "att"), None, None, None),
            P(("grp", "att"), "dev", None, None, None),
            P(),
            P(None, ("att", "dev")),
            P(None, ("att", "dev")),
            P(("att", "dev"), None),
        ),
        out_specs=P(("grp", "att"), "dev", None, None, None),
        check_vma=False,
    )
```

```python
import functools

import jax
import jax.numpy as jnp
from jax import lax
from jax.experimental import pallas as pl
from jax.experimental.pallas import tpu as pltpu
from jax.sharding import PartitionSpec as P

KV_HEADS = 4
MIB = 1 << 20
LONG = 20000000000
ATTC = 3 * LONG
RELC = 0
STAGEC = 1000000000
DOWNC = 10000000000
SLIM = 4
LOG2E = 1.4426950408889634
VMEM = pl.BlockSpec(memory_space=pltpu.VMEM)
HBM = pl.BlockSpec(memory_space=pltpu.HBM)


def params(limit=1 * MIB):
    return pltpu.CompilerParams(vmem_limit_bytes=limit)


def in_hbm(x):
    return pltpu.with_memory_space_constraint(x, pltpu.HBM)


def cost(flops, bytes_accessed):
    return pl.CostEstimate(flops=flops, bytes_accessed=bytes_accessed, transcendentals=0)


def peer(offset):
    return lax.axis_index("dev") ^ offset


def head_start(offset, width):
    return pl.multiple_of(lax.rem(peer(offset), KV_HEADS) * width, width)


def block_start(devices, offset, rows):
    if devices == KV_HEADS:
        return 0
    return pl.multiple_of(peer(offset) // KV_HEADS * rows, rows)


def column_tiles(units, tile=256):
    return [slice(c, min(c + tile, units)) for c in range(0, units, tile)]


def attend_kernel(devices, len_in, q_in, k_in, v_in, kn_in, vn_in, res_in, out_ref, *scratch):
    len_ref, q_ref, k_ref, v_ref, kn_ref, vn_ref, res_ref, len_sem, small_sem, cache_sem = scratch
    rows, width = q_ref.shape
    head = kn_ref.shape[-1]
    heads = width // head
    cache = k_ref.shape[0] // rows
    halves = cache_sem.shape[1]
    part = rows // halves
    groups = part // 8
    block = lax.axis_index("dev") // KV_HEADS if devices > KV_HEADS else 0
    per_batch = len_ref.shape[-1]
    factor = head ** (-0.5) * LOG2E

    lengths = pltpu.make_async_copy(len_in, len_ref, len_sem)
    small = [
        pltpu.make_async_copy(source, target, small_sem.at[n])
        for n, (source, target) in enumerate(((q_in, q_ref), (kn_in, kn_ref), (vn_in, vn_ref), (res_in, res_ref)))
    ]
    cached = []
    for h in range(halves):
        span = pl.ds(h * part * cache, part * cache)
        cached.append(
            [
                pltpu.make_async_copy(source.at[span], target.at[span], cache_sem.at[n, h])
                for n, (source, target) in enumerate(((k_in, k_ref), (v_in, v_ref)))
            ]
        )
    lengths.start()
    small[0].start()
    small[1].start()
    for pair in cached:
        for copy in pair:
            copy.start()
    small[2].start()
    small[3].start()

    relative = lax.broadcasted_iota(jnp.int32, (8, 8 * cache), 1)
    relative = relative - cache * lax.broadcasted_iota(jnp.int32, (8, 8 * cache), 0)
    relative = jnp.where(relative < 0, cache, relative)
    sub = lax.broadcasted_iota(jnp.int32, (8, 128), 0)
    lengths.wait()
    small[0].wait()
    small[1].wait()
    for h in range(halves):
        stripe = slice(h * part, (h + 1) * part)
        wide = q_ref[stripe, :].astype(jnp.float32)
        fresh_keys = kn_ref[stripe, :].astype(jnp.float32)
        spread, keys_spread, biases = [], [], []
        for g in range(groups):
            own = slice(8 * g, 8 * g + 8)
            spread += [wide[own, i * head : (i + 1) * head] for i in range(heads)]
            keys_spread += [fresh_keys[own]] * heads
            limit = jnp.zeros((8, 128), jnp.int32)
            for r in range(8):
                row = h * part + 8 * g + r
                limit = jnp.where(sub == r, len_ref[block, row // per_batch, row % per_batch], limit)
            limit = jnp.concatenate([limit] * (8 * cache // 128), axis=1)
            bias = jnp.where(relative < limit, 0.0, -1e30)
            biases.append(jnp.concatenate([bias] * heads, axis=0))
        q = jnp.concatenate(spread, axis=0)
        fresh = jnp.sum(q * jnp.concatenate(keys_spread, axis=0), axis=-1, keepdims=True)
        q = q.astype(jnp.bfloat16)
        if h == 0:
            small[2].wait()
            small[3].wait()
        for copy in cached[h]:
            copy.wait()
        scores = []
        span = 8 * cache
        for g in range(groups):
            first = (h * groups + g) * span
            scores.append(
                lax.dot_general(
                    q[8 * heads * g : 8 * heads * (g + 1)],
                    k_ref[first : first + span, :],
                    (((1,), (1,)), ((), ())),
                    preferred_element_type=jnp.float32,
                )
                + biases[g]
            )
        scores = jnp.concatenate(scores, axis=0)
        top = jnp.maximum(jnp.max(scores, axis=-1, keepdims=True), fresh)
        weights = jnp.exp2((scores - top) * factor)
        own_weight = jnp.exp2((fresh - top) * factor)
        weights = weights.astype(jnp.bfloat16)
        ones = jnp.ones((span, head), jnp.bfloat16)
        for g in range(groups):
            first = (h * groups + g) * span
            block_rows = slice(8 * heads * g, 8 * heads * (g + 1))
            attended = jnp.dot(
                weights[block_rows], v_ref[first : first + span, :], preferred_element_type=jnp.float32
            )
            total = jnp.dot(weights[block_rows], ones, preferred_element_type=jnp.float32) + own_weight[block_rows]
            own = slice(h * part + 8 * g, h * part + 8 * g + 8)
            fresh_values = vn_ref[h * part : (h + 1) * part, :].astype(jnp.float32)[8 * g : 8 * g + 8]
            attended = attended + own_weight[block_rows] * jnp.concatenate([fresh_values] * heads, axis=0)
            attended = attended / total
            spread[g] = jnp.concatenate([attended[8 * i : 8 * i + 8] for i in range(heads)], axis=1)
        attended = jnp.concatenate(spread[:groups], axis=0)
        out_ref[stripe, :] = (res_ref[stripe, :].astype(jnp.float32) + attended).astype(out_ref.dtype)


def attend(devices, lengths, *arrays):
    query, keys = arrays[:2]
    rows, width = query.shape
    halves = 2
    return pl.pallas_call(
        functools.partial(attend_kernel, devices),
        out_shape=pltpu.VMEM((rows, width), jnp.bfloat16),
        in_specs=[HBM] * (1 + len(arrays)),
        out_specs=VMEM,
        scratch_shapes=[pltpu.SMEM(lengths.shape, lengths.dtype)]
        + [pltpu.VMEM(a.shape, a.dtype) for a in arrays]
        + [
            pltpu.SemaphoreType.DMA,
            pltpu.SemaphoreType.DMA((4,)),
            pltpu.SemaphoreType.DMA((2, halves)),
        ],
        compiler_params=params(5 * MIB),
        cost_estimate=cost(ATTC, 0),
        name="attend",
    )(lengths, *arrays)


def silu_product(gate, up):
    half = 0.5 * gate
    return ((half + half * jnp.tanh(half)) * up).astype(jnp.bfloat16)


def stage_kernel(devices, offsets, first, last, gain_ref, wg_ref, wu_ref, *refs):
    pieces, refs = refs[: 2 * len(offsets)], refs[2 * len(offsets) :]
    if not first:
        gate_in, up_in, square_in = refs[:3]
        refs = refs[3:]
    if last:
        hidden_ref, x_ref = refs[-2:]
    else:
        gate_out, up_out, square_out, x_ref = refs
    rows, width = pieces[0].shape
    units = wg_ref.shape[1]
    many = devices > KV_HEADS
    if many and first:
        for ref in (gate_out, up_out, square_out):
            ref[...] = jnp.zeros_like(ref)
    if many and last:
        gate_out, up_out, square_out = gate_in, up_in, square_in
    if many:
        gate_in, up_in, square_in = gate_out, up_out, square_out
    places, squares = [], []
    for n, offset in enumerate(offsets):
        depth = pl.ds(head_start(offset, width), width)
        places.append((pl.ds(block_start(devices, offset, 2 * rows), 2 * rows), depth))
        gain = gain_ref[depth].astype(jnp.float32).reshape(1, width)
        sums = []
        for side in range(2):
            x = pieces[2 * n + side][...].astype(jnp.float32)
            x_ref[n, side * rows : (side + 1) * rows, :] = (x * gain).astype(jnp.bfloat16)
            sums.append(jnp.sum(x * x, axis=-1, keepdims=True))
        squares.append(jnp.broadcast_to(jnp.concatenate(sums, axis=0), (2 * rows, 128)))

    def product(n, weight, lanes):
        return jnp.dot(x_ref[n], weight[places[n][1], lanes], preferred_element_type=jnp.float32)

    if many:
        for n in range(len(offsets)):
            mine = places[n][0]
            square_out[mine, :] += squares[n]
            for lanes in column_tiles(units):
                gate_out[mine, lanes] += product(n, wg_ref, lanes)
                up_out[mine, lanes] += product(n, wu_ref, lanes)
        if last:
            inverse = lax.rsqrt(square_in[:, :1] / (KV_HEADS * width) + 1e-05)
            for lanes in column_tiles(units):
                hidden_ref[:, lanes] = silu_product(gate_in[:, lanes] * inverse, up_in[:, lanes] * inverse)
        return
    square = sum(squares[1:], squares[0])
    if not first:
        square = square + square_in[...]
    if last:
        inverse = lax.rsqrt(square[:, :1] / (KV_HEADS * width) + 1e-05)
    else:
        square_out[...] = square
    for lanes in column_tiles(units):
        gate = sum(product(n, wg_ref, lanes) for n in range(len(offsets)))
        up = sum(product(n, wu_ref, lanes) for n in range(len(offsets)))
        if not first:
            gate = gate + gate_in[:, lanes]
            up = up + up_in[:, lanes]
        if last:
            hidden_ref[:, lanes] = silu_product(gate * inverse, up * inverse)
        else:
            gate_out[:, lanes] = gate
            up_out[:, lanes] = up


def stage(devices, offsets, pieces, gain, w_gate, w_up, state, final, present):
    rows, width = pieces[0].shape
    units = w_gate.shape[1]
    total = devices // KV_HEADS * 2 * rows
    first, last = not state, final
    arguments = [gain, w_gate, w_up] + list(pieces) + list(state)
    if final:
        arguments += present
    aliases = {}
    if last:
        shapes = [pltpu.VMEM((total, units), jnp.bfloat16)]
    else:
        shapes = [
            pltpu.VMEM((total, units), jnp.float32),
            pltpu.VMEM((total, units), jnp.float32),
            pltpu.VMEM((total, 128), jnp.float32),
        ]
        if not first:
            aliases = {len(arguments) - 3 + n: n for n in range(3)}
    return pl.pallas_call(
        functools.partial(stage_kernel, devices, offsets, first, last),
        out_shape=shapes,
        in_specs=[VMEM] * len(arguments),
        out_specs=[VMEM] * len(shapes),
        input_output_aliases=aliases,
        scratch_shapes=[pltpu.VMEM((len(offsets), 2 * rows, width), jnp.bfloat16)],
        compiler_params=params(devices // KV_HEADS * SLIM * MIB),
        cost_estimate=cost(STAGEC, 0),
        name="stage",
    )(*arguments)


def relay_kernel(piece_ref, *refs):
    refs[-1][...] = piece_ref[...]


def relay(piece, after, present):
    return pl.pallas_call(
        relay_kernel,
        out_shape=pltpu.VMEM(piece.shape, piece.dtype),
        in_specs=[VMEM] + [pl.BlockSpec(memory_space=pl.ANY)] * len(after) + [VMEM] * len(present),
        out_specs=VMEM,
        compiler_params=params(),
        cost_estimate=cost(RELC, 0),
        name="relay",
    )(piece, *after, *present)


def down_kernel(devices, offsets, hidden_ref, weight_ref, *refs):
    keep_ref, send_ref = refs[-2:]
    _, rows, width = keep_ref.shape
    for n, offset in enumerate(offsets):
        mine = pl.ds(block_start(devices, offset, 2 * rows), 2 * rows)
        hidden = hidden_ref[mine, :]
        for lanes in column_tiles(width):
            size = lanes.stop - lanes.start
            column = pl.multiple_of(head_start(offset, width) + lanes.start, size)
            term = jnp.dot(hidden, weight_ref[:, pl.ds(column, size)], preferred_element_type=jnp.float32)
            keep_ref[n, :, lanes] = term[:rows]
            send_ref[n, :, lanes] = term[rows:].astype(jnp.bfloat16)


def down(devices, offsets, hidden, w_down, rows, after=()):
    units, features = w_down.shape
    width = features // KV_HEADS
    shape = (len(offsets), rows, width)
    return pl.pallas_call(
        functools.partial(down_kernel, devices, offsets),
        out_shape=[pltpu.VMEM(shape, jnp.float32), pltpu.VMEM(shape, jnp.bfloat16)],
        in_specs=[VMEM] * 2 + [pl.BlockSpec(memory_space=pl.ANY)] * len(after),
        out_specs=[VMEM] * 2,
        compiler_params=params(),
        cost_estimate=cost(DOWNC, 0),
        name="down",
    )(hidden, w_down, *after)


def fold_kernel(offsets, count, *refs):
    keep_ref, got_ref = refs[:2]
    more, out_refs = refs[2 : 2 + count], refs[-len(offsets) :]
    for n, out_ref in enumerate(out_refs):
        term = keep_ref[n] + got_ref[n].astype(jnp.float32)
        for ref in more:
            term = term + ref[...].astype(jnp.float32)
        out_ref[...] = term.astype(out_ref.dtype)


def fold(offsets, keep, got, more=(), after=(), flops=0):
    _, rows, width = keep.shape
    return pl.pallas_call(
        functools.partial(fold_kernel, offsets, len(more)),
        out_shape=[pltpu.VMEM((rows, width), jnp.float32 if o == 0 else jnp.bfloat16) for o in offsets],
        in_specs=[VMEM] * (2 + len(more)) + [pl.BlockSpec(memory_space=pl.ANY)] * len(after),
        out_specs=[VMEM] * len(offsets),
        compiler_params=params(),
        cost_estimate=cost(flops, 0),
        name="fold",
    )(keep, got, *more, *after)


def finish_kernel(stream_ref, *refs):
    out_ref = refs[-1]
    total = stream_ref[...].astype(jnp.float32)
    for ref in refs[:-1]:
        total = total + ref[...].astype(jnp.float32)
    out_ref[...] = total.astype(out_ref.dtype)


def finish(stream, terms):
    return pl.pallas_call(
        finish_kernel,
        out_shape=jax.ShapeDtypeStruct(stream.shape, jnp.bfloat16),
        compiler_params=params(),
        name="finish",
    )(stream, *terms)


def swap(x):
    return lax.ppermute(x, "att", [(0, 1), (1, 0)])


def exchange(x, offset, devices):
    return lax.ppermute(x, "dev", [(i, i ^ offset) for i in range(devices)])


def shards(
    query, key_cache, value_cache, key_new, value_new, lengths, resid, gain, w_gate, w_up, w_down
):
    devices = lax.axis_size("dev")
    width = query.shape[-1]
    head = key_cache.shape[-1]
    stream = attend(
        devices,
        in_hbm(lengths[0]),
        in_hbm(query.reshape(-1, width)),
        in_hbm(key_cache.reshape(-1, head)),
        in_hbm(value_cache.reshape(-1, head)),
        in_hbm(key_new.reshape(-1, head)),
        in_hbm(value_new.reshape(-1, head)),
        in_hbm(resid.reshape(-1, width)),
    )
    rows = stream.shape[0]
    pieces = {0: stream}
    bit = devices // 2
    while bit:
        for o in tuple(pieces):
            pieces[o ^ bit] = exchange(pieces[o], bit, devices)
        bit //= 2
    groups = [(0,), (2, 1), (3,)] if devices == 4 else [(o,) for o in range(devices)]
    state = ()
    for group in groups:
        arrived = []
        for o in group:
            piece = pieces[o]
            if state and group is groups[-1]:
                piece = relay(piece, state[2:], [w_down])
            elif state:
                piece = relay(piece, state[2:], [])
            arrived += [piece, swap(piece)]
        state = stage(devices, group, arrived, gain, w_gate, w_up, state, group is groups[-1], [])
    hidden = state[0]

    def part(offsets, after=()):
        keep, send = down(devices, offsets, hidden, w_down, rows, after)
        return offsets, keep, swap(send)

    if devices == 4:
        (third,) = fold(*part((3,)))
        relayed = exchange(third, 1, devices)
        second_parts = part((2,))
        nearer_parts = part((1, 0), (third,))
        (second,) = fold(*second_parts, (relayed,), (), LONG)
        first, own = fold(*nearer_parts, (), (second,))
        terms = [own, exchange(first, 1, devices), exchange(second, 2, devices)]
    else:
        terms = {}
        for start in range(devices - 2, -1, -2):
            offsets = (start + 1, start)
            for o, term in zip(offsets, fold(*part(offsets))):
                terms[o] = term if o == 0 else exchange(term, o, devices)
        terms = [terms[o] for o in range(devices)]
    return finish(stream, terms).reshape(query.shape)


def solution(mesh):
    return jax.shard_map(
        shards,
        mesh=mesh,
        in_specs=(
            P(("grp", "att"), "dev", None, None, None),
            P(("grp", "att"), "dev", None, None, None, None),
            P(("grp", "att"), "dev", None, None, None, None),
            P(("grp", "att"), "dev", None, None, None),
            P(("grp", "att"), "dev", None, None, None),
            P(("grp", "att"), None, None, None),
            P(("grp", "att"), "dev", None, None, None),
            P(),
            P(None, ("att", "dev")),
            P(None, ("att", "dev")),
            P(("att", "dev"), None),
        ),
        out_specs=P(("grp", "att"), "dev", None, None, None),
        check_vma=False,
    )
```
